512 devices in a mesh: gx: 8 (over y_lo, core), gy: 8 (over z), gz: 8 (over y_hi, x).
Axes of the slice: x: 4, y: 8 (y_hi: 2, y_lo: 4; y = y_hi * 4 + y_lo), z: 8, core: 2. Of those that a mesh axis runs over, the one named last changes fastest.
Arguments:
- x_act: bfloat16 [1024, 14848], P('gz', ('gx', 'gy')), may hold values from -6 to 6
- d_out: bfloat16 [1024, 14848], P('gz', ('gx', 'gy')), may hold values from -6 to 6
- w_in: bfloat16 [14848, 7424], P(('gx', 'gz'), 'gy'), may hold values from -0.125 to 0.125
- w_out: bfloat16 [7424, 14848], P(('gy', 'gz'), 'gx'), may hold values from -0.0625 to 0.0625
- keep_mask: int32 [1024, 7424], P('gz', 'gy'), may hold values 0 or 1
Outputs:
- d_act: bfloat16 [1024, 14848], P('gz', ('gx', 'gy'))
- d_w_in: bfloat16 [14848, 7424], P(('gx', 'gz'), 'gy')
- d_w_out: bfloat16 [7424, 14848], P(('gy', 'gz'), 'gx')
The draws below stay inside these ranges and needn't reach their ends.
All inputs are finite; a program needn't handle non-finite values. No bound on the sum of `keep_mask` on one device may be relied on, other than what follows from the above.
Results may differ from the reference program's by a relative error of at most 0.0049.
Values may be sent and summed in bfloat16 or wider, within the bound.
No kernel may reach another device: no remote copies, remote signals or barrier semaphores. Data moves between devices by JAX's collectives and lax.ppermute only.
A program may use at most 64 MiB of HBM per device.

```python
import jax
import jax.numpy as jnp
from jax import lax

D = 14848
F = 7424
TOKENS = 1024


def set_ends(entries, own_key, smallest, largest):
    dims = entries.shape
    index_at = [jax.random.randint(jax.random.fold_in(own_key, axis), (), 0, dims[axis]) for axis in range(len(dims))]
    entries = entries.at[tuple(index_at)].set(smallest)
    longest = dims.index(max(dims))
    index_at[longest] = (index_at[longest] + 1) % dims[longest]
    return entries.at[tuple(index_at)].set(largest)


def strengthened(array, rng, source, target, parts, factor):
    def block_of(dim):
        return (jnp.arange(array.shape[dim]) // (array.shape[dim] // parts)).reshape((-1,) + (1,) * (array.ndim - 1 - dim))

    first = jax.random.permutation(rng, parts)[block_of(target)]
    second = (block_of(target) + parts // 2) % parts
    return jnp.where((block_of(source) == first) | (block_of(source) == second), factor * array, array)


def steps_of(stream_key, shape, shards, low, high):
    gain, own = 1.0, jax.random.fold_in(stream_key, 6)
    for dim, parts in shards:
        steps = jnp.exp(jax.random.uniform(jax.random.fold_in(own, dim), (parts,), jnp.float32, low / len(shards), high / len(shards)))
        gain = gain * jnp.repeat(steps, shape[dim] // parts).reshape([-1 if axis == dim else 1 for axis in range(len(shape))])
    return gain


def scatter_about(own_key, extent, spread, most, cuts=(), kind=jnp.bfloat16):
    drawn = jax.random.normal(own_key, extent, jnp.float32) * spread
    if len(cuts) > 0:
        drawn = steps_of(own_key, extent, cuts, -0.22, 0.18) * drawn
    return jnp.clip(drawn, min=-most, max=most).astype(kind)


def bell_draw_with(key, shape, scale, reach, cuts, heavy, held_as=jnp.bfloat16):
    result = scale * jax.random.normal(key, shape, jnp.float32)
    if cuts:
        result = result * steps_of(key, shape, cuts, -0.22, 0.18)
    return jnp.clip(strengthened(result, jax.random.fold_in(key, 3), *heavy), -reach, reach).astype(held_as)


def setup_inputs(seed: int = 0) -> dict:
    key_of = jax.random.split(jax.random.key(seed), 6)
    x_act = scatter_about(key_of[0], (TOKENS, D), 1.0, 6.0, ((0, 8), (1, 64)))
    d_out = scatter_about(key_of[1], (TOKENS, D), 1.0, 6.0, ((0, 8), (1, 64)))
    w_in = bell_draw_with(key_of[2], (D, F), D ** -0.5, 0.125, ((0, 64), (1, 8)), (1, 0, 64, 4.0))
    w_out = scatter_about(key_of[3], (F, D), F ** -0.5, 0.0625, ((0, 64), (1, 8)))
    keep_mask = set_ends((jax.random.randint(key_of[4], (TOKENS, F), 0, 10) < 9).astype(jnp.int32), jax.random.fold_in(key_of[4], 1), 0, 1)
    return dict(x_act=x_act, d_out=d_out, w_in=w_in, w_out=w_out, keep_mask=keep_mask)


def epilogue(hid, d_z, keep_mask):
    keep = keep_mask.astype(jnp.float32) * (1.0 / 0.9)
    cdf = 0.5 * (1.0 + lax.erf(hid * 0.7071067811865476))
    pdf = jnp.exp(-0.5 * hid * hid) * 0.3989422804014327
    z_act = (hid * cdf * keep).astype(jnp.bfloat16)
    d_hid = (d_z * keep * (cdf + hid * pdf)).astype(jnp.bfloat16)
    return z_act, d_hid


def reference(x_act, d_out, w_in, w_out, keep_mask):
    hid = jnp.dot(x_act, w_in, preferred_element_type=jnp.float32)
    d_z = lax.dot_general(d_out, w_out, (((1,), (1,)), ((), ())), preferred_element_type=jnp.float32)
    z_act, d_hid = epilogue(hid, d_z, keep_mask)
    d_act = lax.dot_general(d_hid, w_in, (((1,), (1,)), ((), ())), preferred_element_type=jnp.float32).astype(jnp.bfloat16)
    d_w_in = lax.dot_general(x_act, d_hid, (((0,), (0,)), ((), ())), preferred_element_type=jnp.float32).astype(jnp.bfloat16)
    d_w_out = lax.dot_general(z_act, d_out, (((0,), (0,)), ((), ())), preferred_element_type=jnp.float32).astype(jnp.bfloat16)
    return d_act, d_w_in, d_w_out
```

```python
import jax
import jax.numpy as jnp
from jax import lax
from jax.sharding import Mesh, PartitionSpec as P

F32 = jnp.float32
BF16 = jnp.bfloat16
BLK = 116


def exchange(parts, axis):
    return lax.all_to_all(parts, axis, 0, 0, tiled=True)


def spread(value, axis, n):
    return exchange(jnp.broadcast_to(value[None], (n,) + value.shape), axis)


def swap(value, axis):
    return lax.ppermute(value, axis, [(0, 1), (1, 0)])


def width_to_tokens(inverse):
    pairs = []
    for c in range(2):
        for z in range(8):
            for yh in range(2):
                for x in range(4):
                    c2 = x >> 1
                    z2 = (c ^ c2) * 4 + (z >> 2) * 2 + (x & 1)
                    a = ((c * 8 + z) * 2 + yh) * 4 + x
                    b = ((c2 * 8 + z2) * 2 + yh) * 4 + (z & 3)
                    pairs.append((b, a) if inverse else (a, b))
    return pairs


def keep_pairs():
    pairs = []
    for yl in range(4):
        for c in range(2):
            for x in range(4):
                x2, c2, yl2 = 2 * c + (yl >> 1), x >> 1, (x & 1) * 2 + (yl & 1)
                pairs.append(((yl * 2 + c) * 4 + x, (yl2 * 2 + c2) * 4 + x2))
    return pairs


def dot(spec, a, b):
    return jnp.einsum(spec, a, b, preferred_element_type=F32)


def total(parts):
    return jnp.sum(parts.astype(F32), axis=0)


def in_order(first, mine, other):
    return jnp.where(first, jnp.stack([mine, other]), jnp.stack([other, mine]))


def epilogue(hid, d_z, keep):
    keep = keep * (1.0 / 0.9)
    cdf = 0.5 * (1.0 + lax.erf(hid * 0.7071067811865476))
    pdf = jnp.exp(-0.5 * hid * hid) * 0.3989422804014327
    return (hid * cdf * keep).astype(BF16), (d_z * keep * (cdf + hid * pdf)).astype(BF16)


def local(x_act, d_out, w_in, w_out, keep_mask):
    yl, c, yh = lax.axis_index("yl"), lax.axis_index("c"), lax.axis_index("yh")
    first = yh == 0
    both = jnp.stack([x_act.T, d_out.T])
    both = lax.ppermute(both, ("c", "z", "yh", "x"), width_to_tokens(False))
    both = spread(both, "z", 8)
    acts = both[:, 0].reshape(2, 2, 2, 232, 128)
    grads = spread(both[:, 1], "x", 4).reshape(4, 2, 2, 2, 232, 128)

    w_in2 = in_order(first, w_in, swap(w_in, "yh"))
    w_in2 = jnp.stack([w_in2, swap(w_in2, "c")])
    w_in2 = jnp.pad(w_in2.reshape(2, 2, 232, 2, 4, BLK), ((0, 0),) * 5 + ((0, 12),))
    w_out2 = in_order(first, w_out, swap(w_out, "yh"))
    w_out2 = jnp.stack([w_out2, swap(w_out2, "c")])
    w_out2 = jnp.pad(w_out2, ((0, 0), (0, 0), (0, 12), (0, 0))).reshape(2, 2, 128, 2, 4, 232)

    place = ((yl & 1) * 4 + 2 * c + (yl >> 1)) * BLK
    keep = lax.dynamic_slice(keep_mask, (0, place), (128, BLK)).astype(BF16).T
    keep = jnp.pad(keep, ((0, 12), (0, 0)))
    keep = lax.ppermute(keep, ("yl", "c", "x"), keep_pairs())

    hid = dot("crkabf,crtkn->btafn", w_in2, acts).astype(BF16)
    hid = total(exchange(hid, "x")).astype(BF16).reshape(4, 128, 128)
    d_z = dot("cafrjk,jcrtkn->tafn", w_out2, grads).astype(BF16).reshape(4, 128, 128)
    sums = total(exchange(jnp.stack([hid, d_z], axis=1), "yl"))
    z_act, d_hid = epilogue(sums[0], sums[1], keep.astype(F32))

    both = spread(jnp.stack([z_act, d_hid]), "yl", 4)
    z_act = both[:, 0].reshape(2, 2, 128, 128)
    d_hid = spread(both[:, 1], "x", 4).reshape(4, 2, 2, 128, 128)

    z_act = jnp.stack([z_act, swap(z_act, "c")])
    grads = jnp.stack([grads[:, 0], swap(grads[:, 1], "c")])
    d_wout = dot("ctafn,cjrtkn->afrjk", z_act, grads).reshape(2, 128, 1856)[:, :BLK]
    mine = jnp.where(first, d_wout[0], d_wout[1])
    other = jnp.where(first, d_wout[1], d_wout[0]).astype(BF16)
    d_wout = (mine + swap(other, "yh").astype(F32)).astype(BF16)

    d_act = dot("crkabf,btafn->crtkn", w_in2, d_hid).astype(BF16).reshape(8, 232, 128)
    d_act = total(exchange(d_act, "z")).astype(BF16)
    d_act = lax.ppermute(d_act, ("c", "z", "yh", "x"), width_to_tokens(True)).T

    d_hid = jnp.stack([d_hid, swap(d_hid, "c")])
    acts = jnp.stack([acts[0], swap(acts[1], "c")])
    d_win = dot("crtkn,cbtafn->rkabf", acts, d_hid)[..., :BLK].reshape(2, 232, 928)
    mine = jnp.where(first, d_win[0], d_win[1])
    other = jnp.where(first, d_win[1], d_win[0]).astype(BF16)
    d_win = (mine + swap(other, "yh").astype(F32)).astype(BF16)
    return d_act, d_win, d_wout


def solution(mesh):
    cube = Mesh(mesh.devices.reshape(4, 2, 8, 2, 4), ("yl", "c", "z", "yh", "x"))
    tokens, width = ("yh", "x"), ("yl", "c", "z")
    in_specs = (
        P(tokens, width),
        P(tokens, width),
        P(("yl", "c", "yh", "x"), "z"),
        P(("z", "yh", "x"), ("yl", "c")),
        P(tokens, "z"),
    )
    out_specs = (in_specs[0], in_specs[2], in_specs[3])
    return jax.shard_map(local, mesh=cube, in_specs=in_specs, out_specs=out_specs, check_vma=False)
```

```python
import jax
import jax.numpy as jnp
from jax import lax
from jax.experimental import pallas as pl
from jax.experimental.pallas import tpu as pltpu
from jax.sharding import Mesh, PartitionSpec as P

F32 = jnp.float32
BF16 = jnp.bfloat16
BLK = 116
SUB = 232
HID = 8 * BLK


def call(kernel, out, *args, scratch=(), flops=0):
    arrays = [jax.ShapeDtypeStruct(*o) for o in out]
    moved = sum(a.size * a.dtype.itemsize for a in list(args) + arrays)
    return pl.pallas_call(
        kernel,
        out_shape=arrays,
        scratch_shapes=[pltpu.VMEM(*s) for s in scratch],
        cost_estimate=pl.CostEstimate(flops=flops, bytes_accessed=moved, transcendentals=0),
        compiler_params=pltpu.CompilerParams(vmem_limit_bytes=16 * 2**20),
    )(*args)


def exchange(parts, axis):
    return lax.all_to_all(parts, axis, 0, 0, tiled=True)


def spread(value, axis, n):
    return exchange(jnp.broadcast_to(value[None], (n,) + value.shape), axis)


def swap(value, axis, bit=1):
    n = 4 if axis == "x" else 2
    return lax.ppermute(value, axis, [(i, i ^ bit) for i in range(n)])


def width_to_tokens(inverse):
    pairs = []
    for c in range(2):
        for z in range(8):
            for yh in range(2):
                for x in range(4):
                    c2 = x >> 1
                    z2 = (c ^ c2) * 4 + yh * 2 + (x & 1)
                    a = ((c * 8 + z) * 2 + yh) * 4 + x
                    b = ((c2 * 8 + z2) * 2 + (z >> 2)) * 4 + (z & 3)
                    pairs.append((b, a) if inverse else (a, b))
    return pairs


def keep_pairs():
    pairs = []
    for yl in range(4):
        for c in range(2):
            for yh in range(2):
                for x in range(4):
                    yl2, yh2 = (yl & 2) + yh, yl & 1
                    c2, x2 = x >> 1, c * 2 + (x & 1)
                    a, b = ((yl * 2 + c) * 2 + yh) * 4 + x, ((yl2 * 2 + c2) * 2 + yh2) * 4 + x2
                    pairs.append((a, b))
    return pairs


def mm(a, b, ca, cb):
    return lax.dot_general(a, b, (((ca,), (cb,)), ((), ())), preferred_element_type=F32)


def copies_kernel(x_ref, out_ref):
    value = x_ref[...]
    for i in range(8):
        out_ref[i] = value


def copies2_kernel(x_ref, y_ref, out_ref):
    for k, ref in enumerate((x_ref, y_ref)):
        value = ref[...]
        for i in range(8):
            out_ref[i, k] = value


def hid_kernel(acts, wa, wb, out, rows):
    total = None
    for i, w in enumerate((wa, wb)):
        x = jnp.concatenate([acts[4 * i + t] for t in range(4)], axis=1)
        part = mm(w[...], x, 0, 0)
        total = part if total is None else total + part
    rows[0:HID, :] = total
    live = lax.broadcasted_iota(jnp.int32, (128, 512), 0) < BLK
    for a in range(2):
        for b in range(4):
            block = rows[pl.ds((a * 4 + b) * BLK, 128), :]
            block = jnp.where(live, block, 0.0).astype(BF16)
            for t in range(4):
                out[(b & 2) + (t & 1), 4 * a + 2 * (b & 1) + (t >> 1)] = block[:, 128 * t : 128 * t + 128]


def grad_of(ga, gb):
    cols = [jnp.concatenate([g[j, k] for g in (ga, gb) for k in range(2)], axis=1) for j in range(8)]
    return jnp.concatenate(cols, axis=0)


def place(low, i):
    yh, x = lax.axis_index("yh"), lax.axis_index("x")
    return 4 * ((x // 2) ^ (i // 2)) + 2 * low + (yh ^ (i % 2))


def d_z_kernel(ga, gb, wa, wb, mine, other, blocks):
    c, low = lax.axis_index("c"), lax.axis_index("x") % 2
    grad = grad_of(ga, gb)
    for half, w in ((low, wa), (1 - low, wb)):
        part = mm(w[...], grad, 1, 0)
        part = jnp.concatenate([part, jnp.zeros((128 - BLK, 512), F32)], axis=0)
        for i in range(4):
            blocks[place(half, i)] = part[:, 128 * i : 128 * i + 128]
    for i in range(4):
        mine[i] = blocks[4 * c + i]
        other[i] = blocks[4 * (1 - c) + i]


def sums_kernel(hid, d_z, d_z2, out):
    yh = lax.axis_index("yh")
    out[:, 1] = jnp.zeros((8, 128, 128), BF16)
    for i in range(8):
        total = hid[0, i].astype(F32)
        for s in range(1, 4):
            total = total + hid[s, i].astype(F32)
        out[i, 0] = total.astype(BF16)
    for i in range(4):
        out[4 * yh + i, 1] = (d_z[i] + d_z2[i]).astype(BF16)


def epilogue_kernel(parts, keep_ref, out):
    hid, d_z = (
        sum((parts[s, i].astype(F32) for s in range(1, 8)), parts[0, i].astype(F32))
        for i in range(2)
    )
    keep = keep_ref[...].astype(F32) * (1.0 / 0.9)
    cdf = 0.5 * (1.0 + lax.erf(hid * 0.7071067811865476))
    pdf = jnp.exp(-0.5 * hid * hid) * 0.3989422804014327
    z_act = (hid * cdf * keep).astype(BF16)
    d_hid = (d_z * keep * (cdf + hid * pdf)).astype(BF16)
    for i in range(8):
        out[i, 0] = z_act
        out[i, 1] = d_hid


def split_kernel(both, z_act, d_hid):
    yh = lax.axis_index("yh")
    for i in range(4):
        z_act[i] = both[4 * yh + i, 0]
    for i in range(8):
        for x in range(4):
            d_hid[x, i] = both[i, 1]


def gather_rows(d_hid, rows, at):
    for a in range(2):
        for b in range(4):
            for t in range(4):
                rows[pl.ds((a * 4 + b) * BLK, 128), at + 128 * t : at + 128 * t + 128] = d_hid[
                    (b & 2) + (t & 1), 4 * a + 2 * (b & 1) + (t >> 1)
                ].astype(F32)


def d_act_kernel(d_hid, wa, wb, out, rows):
    gather_rows(d_hid, rows, 0)
    d_hid = rows[0:HID, :].astype(BF16)
    for i, w in enumerate((wa, wb)):
        part = mm(w[...], d_hid, 1, 0).astype(BF16)
        for t in range(4):
            out[4 * i + t] = part[:, 128 * t : 128 * t + 128]


def d_act_sum_kernel(parts, out):
    total = parts[0].astype(F32)
    for s in range(1, 8):
        total = total + parts[s].astype(F32)
    out[...] = total.astype(BF16)


def d_win_kernel(acts, acts2, d_hid, d_hid2, out, rows):
    gather_rows(d_hid, rows, 0)
    gather_rows(d_hid2, rows, 512)
    d_hid = rows[0:HID, :].astype(BF16)
    x = [ref[t] for ref in (acts, acts2) for t in range(4)]
    out[...] = mm(jnp.concatenate(x, axis=1), d_hid, 1, 1).astype(BF16)


def d_wout_kernel(z_act, z_act2, ga, gb, mine, other, z_all):
    c, low = lax.axis_index("c"), lax.axis_index("x") % 2
    for i in range(4):
        z_all[4 * c + i] = z_act[i]
        z_all[4 * (1 - c) + i] = z_act2[i]
    grad = grad_of(ga, gb)
    for half, out in ((low, mine), (1 - low, other)):
        z = [z_all[place(half, i)] for i in range(4)]
        part = mm(jnp.concatenate(z, axis=1), grad, 1, 1)[0:BLK]
        out[...] = part.astype(out.dtype)


def finish_kernel(mine, other, out):
    out[...] = (mine[...] + other[...].astype(F32)).astype(BF16)


def local(x_act, d_out, w_in, w_out, keep_mask):
    yl, c = lax.axis_index("yl"), lax.axis_index("c")
    y_ring = ("yh", "yl")
    hold = lax.optimization_barrier
    flops = 2 * 256 * HID * HID
    block = (128, 128)

    acts = lax.ppermute(x_act.T, ("c", "z", "yh", "x"), width_to_tokens(False))
    (grads,) = call(copies2_kernel, [((8, 2, SUB, 128), BF16)], d_out.T, swap(d_out.T, "yh"))
    grads = exchange(grads, "z")
    w_in2 = swap(w_in, "c")
    at = ((yl & 1) * 4 + 2 * c + (yl >> 1)) * BLK
    keep = lax.dynamic_slice(keep_mask, (0, at), (128, BLK)).astype(BF16).T
    keep = jnp.pad(keep, ((0, 12), (0, 0)))
    keep = lax.ppermute(keep, ("yl", "c", "yh", "x"), keep_pairs())
    (acts,) = call(copies_kernel, [((8, SUB, 128), BF16)], acts)
    acts, grads, keep, w_in2 = hold((acts, grads, keep, w_in2))
    acts = exchange(acts, "z")
    grads2 = swap(grads, "x", 2)
    w_out2 = swap(w_out, "x")

    (hid,) = call(
        hid_kernel, [((4, 8) + block, BF16)], acts, w_in, w_in2, scratch=[((944, 512), F32)], flops=flops
    )
    hid, grads, grads2, w_out2 = hold((hid, grads, grads2, w_out2))
    hid = exchange(hid, "x")
    d_z, d_z2 = call(
        d_z_kernel, [((4,) + block, F32)] * 2, grads, grads2, w_out, w_out2,
        scratch=[((8,) + block, F32)], flops=flops,
    )
    (sums,) = call(sums_kernel, [((8, 2) + block, BF16)], hid, d_z, swap(d_z2, "c"))
    acts2 = swap(acts[4:], "c")
    sums = exchange(sums, y_ring)
    (both,) = call(epilogue_kernel, [((8, 2) + block, BF16)], sums, keep)
    both = exchange(both, y_ring)
    z_act, d_hid = call(split_kernel, [((4,) + block, BF16), ((4, 8) + block, BF16)], both)
    d_hid = exchange(d_hid, "x")

    mine, other = call(
        d_wout_kernel,
        [((BLK, 2 * HID), F32), ((BLK, 2 * HID), BF16)],
        z_act, swap(z_act, "c"), grads, grads2, scratch=[((8,) + block, BF16)], flops=flops,
    )
    d_hid, other, acts2 = hold((d_hid, other, acts2))
    (d_act,) = call(
        d_act_kernel, [((8, SUB, 128), BF16)], d_hid, w_in, w_in2, scratch=[((944, 512), F32)], flops=flops
    )
    d_act = exchange(d_act, "z")
    (d_act,) = call(d_act_sum_kernel, [((SUB, 128), BF16)], d_act)
    d_act = lax.ppermute(d_act, ("c", "z", "yh", "x"), width_to_tokens(True))
    (d_wout,) = call(finish_kernel, [((BLK, 2 * HID), BF16)], mine, swap(other, "x"))

    (d_win,) = call(
        d_win_kernel, [((SUB, HID), BF16)],
        acts[:4], acts2, d_hid, swap(d_hid, "c"), scratch=[((944, 1024), F32)], flops=flops,
    )
    return d_act.T, d_win, d_wout


def solution(mesh):
    cube = Mesh(mesh.devices.reshape(4, 2, 8, 2, 4), ("yl", "c", "z", "yh", "x"))
    tokens, width = ("yh", "x"), ("yl", "c", "z")
    in_specs = (
        P(tokens, width),
        P(tokens, width),
        P(("yl", "c", "yh", "x"), "z"),
        P(("z", "yh", "x"), ("yl", "c")),
        P(tokens, "z"),
    )
    out_specs = (in_specs[0], in_specs[2], in_specs[3])
    return jax.shard_map(local, mesh=cube, in_specs=in_specs, out_specs=out_specs, check_vma=False)
```

```python
import jax
import jax.numpy as jnp
from jax import lax
from jax.experimental import pallas as pl
from jax.experimental.pallas import tpu as pltpu
from jax.sharding import Mesh, PartitionSpec as P

F32 = jnp.float32
BF16 = jnp.bfloat16
BLK = 116
SUB = 232
HID = 8 * BLK


def call(kernel, out, *args, scratch=(), flops=0):
    arrays = [jax.ShapeDtypeStruct(*o) for o in out]
    moved = sum(a.size * a.dtype.itemsize for a in list(args) + arrays)
    return pl.pallas_call(
        kernel,
        out_shape=arrays,
        scratch_shapes=[pltpu.VMEM(*s) for s in scratch],
        cost_estimate=pl.CostEstimate(flops=flops, bytes_accessed=moved, transcendentals=0),
        compiler_params=pltpu.CompilerParams(vmem_limit_bytes=16 * 2**20),
    )(*args)


def exchange(parts, axis):
    return lax.all_to_all(parts, axis, 0, 0, tiled=True)


def spread(value, axis, n):
    return exchange(jnp.broadcast_to(value[None], (n,) + value.shape), axis)


def swap(value, axis, bit=1):
    n = 4 if axis == "x" else 2
    return lax.ppermute(value, axis, [(i, i ^ bit) for i in range(n)])


def width_to_tokens(inverse):
    pairs = []
    for c in range(2):
        for z in range(8):
            for yh in range(2):
                for x in range(4):
                    c2 = x >> 1
                    z2 = (c ^ c2) * 4 + yh * 2 + (x & 1)
                    a = ((c * 8 + z) * 2 + yh) * 4 + x
                    b = ((c2 * 8 + z2) * 2 + (z >> 2)) * 4 + (z & 3)
                    pairs.append((b, a) if inverse else (a, b))
    return pairs


def keep_pairs():
    pairs = []
    for yl in range(4):
        for c in range(2):
            for yh in range(2):
                for x in range(4):
                    yl2, yh2 = (yl & 2) + yh, yl & 1
                    c2, x2 = x >> 1, c * 2 + (x & 1)
                    a, b = ((yl * 2 + c) * 2 + yh) * 4 + x, ((yl2 * 2 + c2) * 2 + yh2) * 4 + x2
                    pairs.append((a, b))
    return pairs


def mm(a, b, ca, cb):
    return lax.dot_general(a, b, (((ca,), (cb,)), ((), ())), preferred_element_type=F32)


def copies_kernel(x_ref, out_ref):
    value = x_ref[...]
    for i in range(8):
        out_ref[i] = value


def copies2_kernel(x_ref, y_ref, out_ref):
    for k, ref in enumerate((x_ref, y_ref)):
        value = ref[...]
        for i in range(8):
            out_ref[i, k] = value


def hid_kernel(acts, wa, wb, out, rows):
    total = None
    for i, w in enumerate((wa, wb)):
        x = jnp.concatenate([acts[4 * i + t] for t in range(4)], axis=1)
        part = mm(w[...], x, 0, 0)
        total = part if total is None else total + part
    rows[0:HID, :] = total
    live = lax.broadcasted_iota(jnp.int32, (128, 512), 0) < BLK
    for a in range(2):
        for b in range(4):
            block = rows[pl.ds((a * 4 + b) * BLK, 128), :]
            block = jnp.where(live, block, 0.0).astype(BF16)
            for t in range(4):
                out[(b & 2) + (t & 1), 4 * a + 2 * (b & 1) + (t >> 1)] = block[:, 128 * t : 128 * t + 128]


def grad_of(ga, gb):
    cols = [jnp.concatenate([g[j, k] for g in (ga, gb) for k in range(2)], axis=1) for j in range(8)]
    return jnp.concatenate(cols, axis=0)


def place(low, i):
    yh, x = lax.axis_index("yh"), lax.axis_index("x")
    return 4 * ((x // 2) ^ (i // 2)) + 2 * low + (yh ^ (i % 2))


def d_z_kernel(ga, gb, wa, wb, mine, other, blocks):
    c, low = lax.axis_index("c"), lax.axis_index("x") % 2
    grad = grad_of(ga, gb)
    for half, w in ((low, wa), (1 - low, wb)):
        part = mm(w[...], grad, 1, 0)
        part = jnp.concatenate([part, jnp.zeros((128 - BLK, 512), F32)], axis=0)
        for i in range(4):
            blocks[place(half, i)] = part[:, 128 * i : 128 * i + 128]
    for i in range(4):
        mine[i] = blocks[4 * c + i]
        other[i] = blocks[4 * (1 - c) + i]


def sums_kernel(hid, d_z, d_z2, out):
    yh = lax.axis_index("yh")
    out[:, 1] = jnp.zeros((8, 128, 128), BF16)
    for i in range(8):
        total = hid[0, i].astype(F32)
        for s in range(1, 4):
            total = total + hid[s, i].astype(F32)
        out[i, 0] = total.astype(BF16)
    for i in range(4):
        out[4 * yh + i, 1] = (d_z[i] + d_z2[i]).astype(BF16)


def epilogue_kernel(parts, keep_ref, out):
    hid, d_z = (
        sum((parts[s, i].astype(F32) for s in range(1, 8)), parts[0, i].astype(F32))
        for i in range(2)
    )
    keep = keep_ref[...].astype(F32) * (1.0 / 0.9)
    cdf = 0.5 * (1.0 + lax.erf(hid * 0.7071067811865476))
    pdf = jnp.exp(-0.5 * hid * hid) * 0.3989422804014327
    z_act = (hid * cdf * keep).astype(BF16)
    d_hid = (d_z * keep * (cdf + hid * pdf)).astype(BF16)
    for i in range(8):
        out[i, 0] = z_act
        out[i, 1] = d_hid


def split_kernel(both, z_act, d_hid):
    yh = lax.axis_index("yh")
    for i in range(4):
        z_act[i] = both[4 * yh + i, 0]
    for i in range(8):
        for x in range(4):
            d_hid[x, i] = both[i, 1]


def gather_rows(d_hid, rows, at):
    for a in range(2):
        for b in range(4):
            for t in range(4):
                rows[pl.ds((a * 4 + b) * BLK, 128), at + 128 * t : at + 128 * t + 128] = d_hid[
                    (b & 2) + (t & 1), 4 * a + 2 * (b & 1) + (t >> 1)
                ].astype(F32)


def d_act_kernel(d_hid, wa, wb, out, rows):
    gather_rows(d_hid, rows, 0)
    d_hid = rows[0:HID, :].astype(BF16)
    for i, w in enumerate((wa, wb)):
        part = mm(w[...], d_hid, 1, 0).astype(BF16)
        for t in range(4):
            out[4 * i + t] = part[:, 128 * t : 128 * t + 128]


def d_act_sum_kernel(parts, out):
    total = parts[0].astype(F32)
    for s in range(1, 8):
        total = total + parts[s].astype(F32)
    out[...] = total.astype(BF16)


def d_win_kernel(acts, acts2, d_hid, d_hid2, out, rows):
    gather_rows(d_hid, rows, 0)
    gather_rows(d_hid2, rows, 512)
    d_hid = rows[0:HID, :].astype(BF16)
    x = [ref[t] for ref in (acts, acts2) for t in range(4)]
    out[...] = mm(jnp.concatenate(x, axis=1), d_hid, 1, 1).astype(BF16)


def d_wout_kernel(z_act, z_act2, ga, gb, mine, other, z_all):
    c, low = lax.axis_index("c"), lax.axis_index("x") % 2
    for i in range(4):
        z_all[4 * c + i] = z_act[i]
        z_all[4 * (1 - c) + i] = z_act2[i]
    grad = grad_of(ga, gb)
    for half, out in ((low, mine), (1 - low, other)):
        z = [z_all[place(half, i)] for i in range(4)]
        part = mm(jnp.concatenate(z, axis=1), grad, 1, 1)[0:BLK]
        out[...] = part.astype(out.dtype)


def finish_kernel(mine, other, out):
    out[...] = (mine[...] + other[...].astype(F32)).astype(BF16)


def local(x_act, d_out, w_in, w_out, keep_mask):
    yl, c = lax.axis_index("yl"), lax.axis_index("c")
    y_ring = ("yh", "yl")
    hold = lax.optimization_barrier
    flops = 2 * 256 * HID * HID
    block = (128, 128)

    acts = lax.ppermute(x_act.T, ("c", "z", "yh", "x"), width_to_tokens(False))
    (grads,) = call(copies2_kernel, [((8, 2, SUB, 128), BF16)], d_out.T, swap(d_out.T, "yh"))
    grads = exchange(grads, "z")
    w_in2 = swap(w_in, "c")
    at = ((yl & 1) * 4 + 2 * c + (yl >> 1)) * BLK
    keep = lax.dynamic_slice(keep_mask, (0, at), (128, BLK)).astype(BF16).T
    keep = jnp.pad(keep, ((0, 12), (0, 0)))
    keep = lax.ppermute(keep, ("yl", "c", "yh", "x"), keep_pairs())
    (acts,) = call(copies_kernel, [((8, SUB, 128), BF16)], acts)
    w_out2 = swap(w_out, "x")
    acts, grads, keep, w_in2, w_out2 = hold((acts, grads, keep, w_in2, w_out2))
    acts = exchange(acts, "z")
    grads2 = swap(grads, "x", 2)

    (hid,) = call(
        hid_kernel, [((4, 8) + block, BF16)], acts, w_in, w_in2, scratch=[((944, 512), F32)], flops=flops
    )
    hid, grads, grads2 = hold((hid, grads, grads2))
    hid = exchange(hid, "x")
    d_z, d_z2 = call(
        d_z_kernel, [((4,) + block, F32)] * 2, grads, grads2, w_out, w_out2,
        scratch=[((8,) + block, F32)], flops=flops,
    )
    (sums,) = call(sums_kernel, [((8, 2) + block, BF16)], hid, d_z, swap(d_z2, "c"))
    acts2 = swap(acts[4:], "c")
    sums = exchange(sums, y_ring)
    (both,) = call(epilogue_kernel, [((8, 2) + block, BF16)], sums, keep)
    both = exchange(both, y_ring)
    z_act, d_hid = call(split_kernel, [((4,) + block, BF16), ((4, 8) + block, BF16)], both)
    d_hid = exchange(d_hid, "x")

    mine, other = call(
        d_wout_kernel,
        [((BLK, 2 * HID), F32), ((BLK, 2 * HID), BF16)],
        z_act, swap(z_act, "c"), grads, grads2, scratch=[((8,) + block, BF16)], flops=flops,
    )
    d_hid, other, acts2 = hold((d_hid, other, acts2))
    (d_act,) = call(
        d_act_kernel, [((8, SUB, 128), BF16)], d_hid, w_in, w_in2, scratch=[((944, 512), F32)], flops=flops
    )
    d_act = exchange(d_act, "z")
    (d_act,) = call(d_act_sum_kernel, [((SUB, 128), BF16)], d_act)
    (d_win,) = call(
        d_win_kernel, [((SUB, HID), BF16)],
        acts[:4], acts2, d_hid, swap(d_hid, "c"), scratch=[((944, 1024), F32)], flops=flops,
    )
    d_act, d_win = hold((d_act, d_win))
    d_act = lax.ppermute(d_act, ("c", "z", "yh", "x"), width_to_tokens(True))
    (d_wout,) = call(finish_kernel, [((BLK, 2 * HID), BF16)], mine, swap(other, "x"))
    return d_act.T, d_win, d_wout


def solution(mesh):
    cube = Mesh(mesh.devices.reshape(4, 2, 8, 2, 4), ("yl", "c", "z", "yh", "x"))
    tokens, width = ("yh", "x"), ("yl", "c", "z")
    in_specs = (
        P(tokens, width),
        P(tokens, width),
        P(("yl", "c", "yh", "x"), "z"),
        P(("z", "yh", "x"), ("yl", "c")),
        P(tokens, "z"),
    )
    out_specs = (in_specs[0], in_specs[2], in_specs[3])
    return jax.shard_map(local, mesh=cube, in_specs=in_specs, out_specs=out_specs, check_vma=False)
```

```python
import jax
import jax.numpy as jnp
from jax import lax
from jax.experimental import pallas as pl
from jax.experimental.pallas import tpu as pltpu
from jax.sharding import Mesh, PartitionSpec as P

F32 = jnp.float32
BF16 = jnp.bfloat16
BLK = 116
SUB = 232
HID = 8 * BLK


def call(kernel, out, *args, scratch=(), flops=0):
    arrays = [jax.ShapeDtypeStruct(*o) for o in out]
    moved = sum(a.size * a.dtype.itemsize for a in list(args) + arrays)
    return pl.pallas_call(
        kernel,
        out_shape=arrays,
        scratch_shapes=[pltpu.VMEM(*s) for s in scratch],
        cost_estimate=pl.CostEstimate(flops=flops, bytes_accessed=moved, transcendentals=0),
        compiler_params=pltpu.CompilerParams(vmem_limit_bytes=16 * 2**20),
    )(*args)


def exchange(parts, axis):
    return lax.all_to_all(parts, axis, 0, 0, tiled=True)


def spread(value, axis, n):
    return exchange(jnp.broadcast_to(value[None], (n,) + value.shape), axis)


def swap(value, axis, bit=1):
    n = 4 if axis == "x" else 2
    return lax.ppermute(value, axis, [(i, i ^ bit) for i in range(n)])


def width_to_tokens(inverse):
    pairs = []
    for c in range(2):
        for z in range(8):
            for yh in range(2):
                for x in range(4):
                    c2 = x >> 1
                    z2 = (c ^ c2) * 4 + yh * 2 + (x & 1)
                    a = ((c * 8 + z) * 2 + yh) * 4 + x
                    b = ((c2 * 8 + z2) * 2 + (z >> 2)) * 4 + (z & 3)
                    pairs.append((b, a) if inverse else (a, b))
    return pairs


def keep_pairs():
    pairs = []
    for yl in range(4):
        for c in range(2):
            for yh in range(2):
                for x in range(4):
                    yl2, yh2 = (yl & 2) + yh, yl & 1
                    c2, x2 = x >> 1, c * 2 + (x & 1)
                    a, b = ((yl * 2 + c) * 2 + yh) * 4 + x, ((yl2 * 2 + c2) * 2 + yh2) * 4 + x2
                    pairs.append((a, b))
    return pairs


def mm(a, b, ca, cb):
    return lax.dot_general(a, b, (((ca,), (cb,)), ((), ())), preferred_element_type=F32)


def copies_kernel(x_ref, out_ref):
    value = x_ref[...]
    for i in range(8):
        out_ref[i] = value


def copies2_kernel(x_ref, y_ref, out_ref):
    for k, ref in enumerate((x_ref, y_ref)):
        value = ref[...]
        for i in range(8):
            out_ref[i, k] = value


def hid_kernel(acts, wa, wb, out, rows):
    total = None
    for i, w in enumerate((wa, wb)):
        x = jnp.concatenate([acts[4 * i + t] for t in range(4)], axis=1)
        part = mm(w[...], x, 0, 0)
        total = part if total is None else total + part
    rows[0:HID, :] = total
    live = lax.broadcasted_iota(jnp.int32, (128, 512), 0) < BLK
    for a in range(2):
        for b in range(4):
            block = rows[pl.ds((a * 4 + b) * BLK, 128), :]
            block = jnp.where(live, block, 0.0).astype(BF16)
            for t in range(4):
                out[(b & 2) + (t & 1), 4 * a + 2 * (b & 1) + (t >> 1)] = block[:, 128 * t : 128 * t + 128]


def grad_of(ga, gb):
    cols = [jnp.concatenate([g[j, k] for g in (ga, gb) for k in range(2)], axis=1) for j in range(8)]
    return jnp.concatenate(cols, axis=0)


def place(low, i):
    yh, x = lax.axis_index("yh"), lax.axis_index("x")
    return 4 * ((x // 2) ^ (i // 2)) + 2 * low + (yh ^ (i % 2))


def d_z_kernel(ga, gb, wa, wb, mine, other, blocks):
    c, low = lax.axis_index("c"), lax.axis_index("x") % 2
    grad = grad_of(ga, gb)
    for half, w in ((low, wa), (1 - low, wb)):
        part = mm(w[...], grad, 1, 0)
        part = jnp.concatenate([part, jnp.zeros((128 - BLK, 512), F32)], axis=0)
        for i in range(4):
            blocks[place(half, i)] = part[:, 128 * i : 128 * i + 128]
    for i in range(4):
        mine[i] = blocks[4 * c + i]
        other[i] = blocks[4 * (1 - c) + i]


def sums_kernel(hid, d_z, d_z2, out):
    yh = lax.axis_index("yh")
    out[:, 1] = jnp.zeros((8, 128, 128), BF16)
    for i in range(8):
        total = hid[0, i].astype(F32)
        for s in range(1, 4):
            total = total + hid[s, i].astype(F32)
        out[i, 0] = total.astype(BF16)
    for i in range(4):
        out[4 * yh + i, 1] = (d_z[i] + d_z2[i]).astype(BF16)


def epilogue_kernel(parts, keep_ref, out):
    hid, d_z = (
        sum((parts[s, i].astype(F32) for s in range(1, 8)), parts[0, i].astype(F32))
        for i in range(2)
    )
    keep = keep_ref[...].astype(F32) * (1.0 / 0.9)
    cdf = 0.5 * (1.0 + lax.erf(hid * 0.7071067811865476))
    pdf = jnp.exp(-0.5 * hid * hid) * 0.3989422804014327
    z_act = (hid * cdf * keep).astype(BF16)
    d_hid = (d_z * keep * (cdf + hid * pdf)).astype(BF16)
    for i in range(8):
        out[i, 0] = z_act
        out[i, 1] = d_hid


def split_kernel(both, z_act, d_hid):
    yh = lax.axis_index("yh")
    for i in range(4):
        z_act[i] = both[4 * yh + i, 0]
    for i in range(8):
        for x in range(4):
            d_hid[x, i] = both[i, 1]


def gather_rows(d_hid, rows, at):
    for a in range(2):
        for b in range(4):
            for t in range(4):
                rows[pl.ds((a * 4 + b) * BLK, 128), at + 128 * t : at + 128 * t + 128] = d_hid[
                    (b & 2) + (t & 1), 4 * a + 2 * (b & 1) + (t >> 1)
                ].astype(F32)


def d_act_kernel(d_hid, wa, wb, out, rows):
    gather_rows(d_hid, rows, 0)
    d_hid = rows[0:HID, :].astype(BF16)
    for i, w in enumerate((wa, wb)):
        part = mm(w[...], d_hid, 1, 0).astype(BF16)
        for t in range(4):
            out[4 * i + t] = part[:, 128 * t : 128 * t + 128]


def d_act_sum_kernel(parts, out):
    total = parts[0].astype(F32)
    for s in range(1, 8):
        total = total + parts[s].astype(F32)
    out[...] = total.astype(BF16)


def d_win_kernel(acts, d_hid, mine, other, rows):
    gather_rows(d_hid, rows, 0)
    d_hid = rows[0:HID, :].astype(BF16)
    for i, out in enumerate((mine, other)):
        x = jnp.concatenate([acts[4 * i + t] for t in range(4)], axis=1)
        out[...] = mm(x, d_hid, 1, 1).astype(out.dtype)


def d_wout_kernel(z_act, z_act2, ga, gb, mine, other, z_all):
    c, low = lax.axis_index("c"), lax.axis_index("x") % 2
    for i in range(4):
        z_all[4 * c + i] = z_act[i]
        z_all[4 * (1 - c) + i] = z_act2[i]
    grad = grad_of(ga, gb)
    for half, out in ((low, mine), (1 - low, other)):
        z = [z_all[place(half, i)] for i in range(4)]
        part = mm(jnp.concatenate(z, axis=1), grad, 1, 1)[0:BLK]
        out[...] = part.astype(out.dtype)


def finish_kernel(mine, other, out):
    out[...] = (mine[...] + other[...].astype(F32)).astype(BF16)


def local(x_act, d_out, w_in, w_out, keep_mask):
    yl, c = lax.axis_index("yl"), lax.axis_index("c")
    y_ring = ("yh", "yl")
    hold = lax.optimization_barrier
    flops = 2 * 256 * HID * HID
    block = (128, 128)

    acts = lax.ppermute(x_act.T, ("c", "z", "yh", "x"), width_to_tokens(False))
    (grads,) = call(copies2_kernel, [((8, 2, SUB, 128), BF16)], d_out.T, swap(d_out.T, "yh"))
    grads = exchange(grads, "z")
    w_in2 = swap(w_in, "c")
    at = ((yl & 1) * 4 + 2 * c + (yl >> 1)) * BLK
    keep = lax.dynamic_slice(keep_mask, (0, at), (128, BLK)).astype(BF16).T
    keep = jnp.pad(keep, ((0, 12), (0, 0)))
    keep = lax.ppermute(keep, ("yl", "c", "yh", "x"), keep_pairs())
    (acts,) = call(copies_kernel, [((8, SUB, 128), BF16)], acts)
    w_out2 = swap(w_out, "x")
    acts, grads, keep, w_in2, w_out2 = hold((acts, grads, keep, w_in2, w_out2))
    acts = exchange(acts, "z")
    grads2 = swap(grads, "x", 2)

    (hid,) = call(
        hid_kernel, [((4, 8) + block, BF16)], acts, w_in, w_in2, scratch=[((944, 512), F32)], flops=flops
    )
    hid, grads, grads2 = hold((hid, grads, grads2))
    hid = exchange(hid, "x")
    d_z, d_z2 = call(
        d_z_kernel, [((4,) + block, F32)] * 2, grads, grads2, w_out, w_out2,
        scratch=[((8,) + block, F32)], flops=flops,
    )
    (sums,) = call(sums_kernel, [((8, 2) + block, BF16)], hid, d_z, swap(d_z2, "c"))
    sums = exchange(sums, y_ring)
    (both,) = call(epilogue_kernel, [((8, 2) + block, BF16)], sums, keep)
    both = exchange(both, y_ring)
    z_act, d_hid = call(split_kernel, [((4,) + block, BF16), ((4, 8) + block, BF16)], both)
    d_hid = exchange(d_hid, "x")

    mine, other = call(
        d_wout_kernel,
        [((BLK, 2 * HID), F32), ((BLK, 2 * HID), BF16)],
        z_act, swap(z_act, "c"), grads, grads2, scratch=[((8,) + block, BF16)], flops=flops,
    )
    d_hid, other = hold((d_hid, other))
    (d_act,) = call(
        d_act_kernel, [((8, SUB, 128), BF16)], d_hid, w_in, w_in2, scratch=[((944, 512), F32)], flops=flops
    )
    d_act = exchange(d_act, "z")
    mine_in, other_in = call(
        d_win_kernel, [((SUB, HID), F32), ((SUB, HID), BF16)],
        acts, d_hid, scratch=[((944, 512), F32)], flops=flops,
    )
    (d_win,) = call(finish_kernel, [((SUB, HID), BF16)], mine_in, swap(other_in, "c"))
    d_act, d_win = hold((d_act, d_win))
    (d_act,) = call(d_act_sum_kernel, [((SUB, 128), BF16)], d_act)
    d_act = lax.ppermute(d_act, ("c", "z", "yh", "x"), width_to_tokens(True))
    (d_wout,) = call(finish_kernel, [((BLK, 2 * HID), BF16)], mine, swap(other, "x"))
    return d_act.T, d_win, d_wout


def solution(mesh):
    cube = Mesh(mesh.devices.reshape(4, 2, 8, 2, 4), ("yl", "c", "z", "yh", "x"))
    tokens, width = ("yh", "x"), ("yl", "c", "z")
    in_specs = (
        P(tokens, width),
        P(tokens, width),
        P(("yl", "c", "yh", "x"), "z"),
        P(("z", "yh", "x"), ("yl", "c")),
        P(tokens, "z"),
    )
    out_specs = (in_specs[0], in_specs[2], in_specs[3])
    return jax.shard_map(local, mesh=cube, in_specs=in_specs, out_specs=out_specs, check_vma=False)
```

```python
import jax
import jax.numpy as jnp
from jax import lax
from jax.experimental import pallas as pl
from jax.experimental.pallas import tpu as pltpu
from jax.sharding import Mesh, PartitionSpec as P

F32 = jnp.float32
BF16 = jnp.bfloat16
BLK = 116
PAD = 120
SUB = 232
HID = 8 * BLK


def call(kernel, out, *args, scratch=(), flops=0):
    arrays = [jax.ShapeDtypeStruct(*o) for o in out]
    moved = sum(a.size * a.dtype.itemsize for a in list(args) + arrays)
    return pl.pallas_call(
        kernel,
        out_shape=arrays,
        scratch_shapes=[pltpu.VMEM(*s) for s in scratch],
        cost_estimate=pl.CostEstimate(flops=flops, bytes_accessed=moved, transcendentals=0),
        compiler_params=pltpu.CompilerParams(vmem_limit_bytes=16 * 2**20),
    )(*args)


def exchange(parts, axis):
    return lax.all_to_all(parts, axis, 0, 0, tiled=True)


def spread(value, axis, n):
    return exchange(jnp.broadcast_to(value[None], (n,) + value.shape), axis)


def swap(value, axis, bit=1):
    n = 4 if axis == "x" else 2
    return lax.ppermute(value, axis, [(i, i ^ bit) for i in range(n)])


def width_to_tokens(inverse):
    pairs = []
    for c in range(2):
        for z in range(8):
            for yh in range(2):
                for x in range(4):
                    c2 = x >> 1
                    z2 = (c ^ c2) * 4 + yh * 2 + (x & 1)
                    a = ((c * 8 + z) * 2 + yh) * 4 + x
                    b = ((c2 * 8 + z2) * 2 + (z >> 2)) * 4 + (z & 3)
                    pairs.append((b, a) if inverse else (a, b))
    return pairs


def keep_pairs():
    pairs = []
    for yl in range(4):
        for c in range(2):
            for yh in range(2):
                for x in range(4):
                    yl2, yh2 = (yl & 2) + yh, yl & 1
                    c2, x2 = x >> 1, c * 2 + (x & 1)
                    a, b = ((yl * 2 + c) * 2 + yh) * 4 + x, ((yl2 * 2 + c2) * 2 + yh2) * 4 + x2
                    pairs.append((a, b))
    return pairs


def mm(a, b, ca, cb):
    return lax.dot_general(a, b, (((ca,), (cb,)), ((), ())), preferred_element_type=F32)


def copies_kernel(x_ref, out_ref):
    value = x_ref[...]
    for i in range(8):
        out_ref[i] = value


def copies2_kernel(x_ref, y_ref, out_ref):
    for k, ref in enumerate((x_ref, y_ref)):
        value = ref[...]
        for i in range(8):
            out_ref[i, k] = value


def hid_kernel(acts, wa, wb, out, rows):
    total = None
    for i, w in enumerate((wa, wb)):
        x = jnp.concatenate([acts[4 * i + t] for t in range(4)], axis=1)
        part = mm(w[...], x, 0, 0)
        total = part if total is None else total + part
    rows[0:HID, :] = total
    live = lax.broadcasted_iota(jnp.int32, (PAD, 512), 0) < BLK
    for a in range(2):
        for b in range(4):
            block = rows[pl.ds((a * 4 + b) * BLK, PAD), :]
            block = jnp.where(live, block, 0.0).astype(BF16)
            for t in range(4):
                out[(b & 2) + (t & 1), 4 * a + 2 * (b & 1) + (t >> 1)] = block[:, 128 * t : 128 * t + 128]


def grad_of(ga, gb):
    cols = [jnp.concatenate([g[j, k] for g in (ga, gb) for k in range(2)], axis=1) for j in range(8)]
    return jnp.concatenate(cols, axis=0)


def place(low, i):
    yh, x = lax.axis_index("yh"), lax.axis_index("x")
    return 4 * ((x // 2) ^ (i // 2)) + 2 * low + (yh ^ (i % 2))


def d_z_kernel(ga, gb, wa, wb, mine, other, blocks):
    c, low = lax.axis_index("c"), lax.axis_index("x") % 2
    grad = grad_of(ga, gb)
    for half, w in ((low, wa), (1 - low, wb)):
        part = mm(w[...], grad, 1, 0)
        part = jnp.concatenate([part, jnp.zeros((PAD - BLK, 512), F32)], axis=0)
        for i in range(4):
            blocks[place(half, i)] = part[:, 128 * i : 128 * i + 128]
    for i in range(4):
        mine[i] = blocks[4 * c + i]
        other[i] = blocks[4 * (1 - c) + i]


def sums_kernel(hid, d_z, d_z2, out):
    yh = lax.axis_index("yh")
    out[:, 1] = jnp.zeros((8, PAD, 128), BF16)
    for i in range(8):
        total = hid[0, i].astype(F32)
        for s in range(1, 4):
            total = total + hid[s, i].astype(F32)
        out[i, 0] = total.astype(BF16)
    for i in range(4):
        out[4 * yh + i, 1] = (d_z[i] + d_z2[i]).astype(BF16)


def epilogue_kernel(parts, keep_ref, out):
    hid, d_z = (
        sum((parts[s, i].astype(F32) for s in range(1, 8)), parts[0, i].astype(F32))
        for i in range(2)
    )
    keep = keep_ref[...].astype(F32) * (1.0 / 0.9)
    cdf = 0.5 * (1.0 + lax.erf(hid * 0.7071067811865476))
    pdf = jnp.exp(-0.5 * hid * hid) * 0.3989422804014327
    z_act = (hid * cdf * keep).astype(BF16)
    d_hid = (d_z * keep * (cdf + hid * pdf)).astype(BF16)
    for i in range(8):
        out[i, 0] = z_act
        out[i, 1] = d_hid


def split_kernel(both, z_act, d_hid):
    yh = lax.axis_index("yh")
    for i in range(4):
        z_act[i] = both[4 * yh + i, 0]
    for i in range(8):
        for x in range(4):
            d_hid[x, i] = both[i, 1]


def gather_rows(d_hid, rows, at):
    for a in range(2):
        for b in range(4):
            for t in range(4):
                rows[pl.ds((a * 4 + b) * BLK, PAD), at + 128 * t : at + 128 * t + 128] = d_hid[
                    (b & 2) + (t & 1), 4 * a + 2 * (b & 1) + (t >> 1)
                ].astype(F32)


def d_act_kernel(d_hid, wa, wb, out, rows):
    gather_rows(d_hid, rows, 0)
    d_hid = rows[0:HID, :].astype(BF16)
    for i, w in enumerate((wa, wb)):
        part = mm(w[...], d_hid, 1, 0).astype(BF16)
        for t in range(4):
            out[4 * i + t] = part[:, 128 * t : 128 * t + 128]


def d_act_sum_kernel(parts, out):
    total = parts[0].astype(F32)
    for s in range(1, 8):
        total = total + parts[s].astype(F32)
    out[...] = total.astype(BF16)


def d_win_kernel(acts, d_hid, mine, other, rows):
    gather_rows(d_hid, rows, 0)
    d_hid = rows[0:HID, :].astype(BF16)
    for i, out in enumerate((mine, other)):
        x = jnp.concatenate([acts[4 * i + t] for t in range(4)], axis=1)
        out[...] = mm(x, d_hid, 1, 1).astype(out.dtype)


def d_wout_kernel(z_act, z_act2, ga, gb, mine, other, z_all):
    c, low = lax.axis_index("c"), lax.axis_index("x") % 2
    for i in range(4):
        z_all[4 * c + i] = z_act[i]
        z_all[4 * (1 - c) + i] = z_act2[i]
    grad = grad_of(ga, gb)
    for half, out in ((low, mine), (1 - low, other)):
        z = [z_all[place(half, i)] for i in range(4)]
        part = mm(jnp.concatenate(z, axis=1), grad, 1, 1)[0:BLK]
        out[...] = part.astype(out.dtype)


def finish_kernel(mine, other, out):
    out[...] = (mine[...] + other[...].astype(F32)).astype(BF16)


def local(x_act, d_out, w_in, w_out, keep_mask):
    yl, c = lax.axis_index("yl"), lax.axis_index("c")
    y_ring = ("yh", "yl")
    hold = lax.optimization_barrier
    flops = 2 * 256 * HID * HID
    block = (PAD, 128)

    acts = lax.ppermute(x_act.T, ("c", "z", "yh", "x"), width_to_tokens(False))
    (grads,) = call(copies2_kernel, [((8, 2, SUB, 128), BF16)], d_out.T, swap(d_out.T, "yh"))
    grads = exchange(grads, "z")
    w_in2 = swap(w_in, "c")
    at = ((yl & 1) * 4 + 2 * c + (yl >> 1)) * BLK
    keep = lax.dynamic_slice(keep_mask, (0, at), (128, BLK)).astype(BF16).T
    keep = jnp.pad(keep, ((0, PAD - BLK), (0, 0)))
    keep = lax.ppermute(keep, ("yl", "c", "yh", "x"), keep_pairs())
    (acts,) = call(copies_kernel, [((8, SUB, 128), BF16)], acts)
    w_out2 = swap(w_out, "x")
    acts, grads, keep, w_in2, w_out2 = hold((acts, grads, keep, w_in2, w_out2))
    acts = exchange(acts, "z")
    grads2 = swap(grads, "x", 2)

    (hid,) = call(
        hid_kernel, [((4, 8) + block, BF16)], acts, w_in, w_in2, scratch=[((944, 512), F32)], flops=flops
    )
    hid, grads, grads2 = hold((hid, grads, grads2))
    hid = exchange(hid, "x")
    d_z, d_z2 = call(
        d_z_kernel, [((4,) + block, F32)] * 2, grads, grads2, w_out, w_out2,
        scratch=[((8,) + block, F32)], flops=flops,
    )
    (sums,) = call(sums_kernel, [((8, 2) + block, BF16)], hid, d_z, swap(d_z2, "c"))
    sums = exchange(sums, y_ring)
    (both,) = call(epilogue_kernel, [((8, 2) + block, BF16)], sums, keep)
    both = exchange(both, y_ring)
    z_act, d_hid = call(split_kernel, [((4,) + block, BF16), ((4, 8) + block, BF16)], both)
    d_hid = exchange(d_hid, "x")

    mine, other = call(
        d_wout_kernel,
        [((BLK, 2 * HID), F32), ((BLK, 2 * HID), BF16)],
        z_act, swap(z_act, "c"), grads, grads2, scratch=[((8,) + block, BF16)], flops=flops,
    )
    d_hid, other = hold((d_hid, other))
    (d_act,) = call(
        d_act_kernel, [((8, SUB, 128), BF16)], d_hid, w_in, w_in2, scratch=[((944, 512), F32)], flops=flops
    )
    d_act = exchange(d_act, "z")
    mine_in, other_in = call(
        d_win_kernel, [((SUB, HID), F32), ((SUB, HID), BF16)],
        acts, d_hid, scratch=[((944, 512), F32)], flops=flops,
    )
    (d_win,) = call(finish_kernel, [((SUB, HID), BF16)], mine_in, swap(other_in, "c"))
    d_act, d_win = hold((d_act, d_win))
    (d_act,) = call(d_act_sum_kernel, [((SUB, 128), BF16)], d_act)
    d_act = lax.ppermute(d_act, ("c", "z", "yh", "x"), width_to_tokens(True))
    (d_wout,) = call(finish_kernel, [((BLK, 2 * HID), BF16)], mine, swap(other, "x"))
    return d_act.T, d_win, d_wout


def solution(mesh):
    cube = Mesh(mesh.devices.reshape(4, 2, 8, 2, 4), ("yl", "c", "z", "yh", "x"))
    tokens, width = ("yh", "x"), ("yl", "c", "z")
    in_specs = (
        P(tokens, width),
        P(tokens, width),
        P(("yl", "c", "yh", "x"), "z"),
        P(("z", "yh", "x"), ("yl", "c")),
        P(tokens, "z"),
    )
    out_specs = (in_specs[0], in_specs[2], in_specs[3])
    return jax.shard_map(local, mesh=cube, in_specs=in_specs, out_specs=out_specs, check_vma=False)
```

```python
import jax
import jax.numpy as jnp
from jax import lax
from jax.experimental import pallas as pl
from jax.experimental.pallas import tpu as pltpu
from jax.sharding import Mesh, PartitionSpec as P

F32 = jnp.float32
BF16 = jnp.bfloat16
BLK = 116
PAD = 120
SUB = 232
HID = 8 * BLK


def call(kernel, out, *args, scratch=(), flops=0):
    arrays = [jax.ShapeDtypeStruct(*o) for o in out]
    moved = sum(a.size * a.dtype.itemsize for a in list(args) + arrays)
    return pl.pallas_call(
        kernel,
        out_shape=arrays,
        scratch_shapes=[pltpu.VMEM(*s) for s in scratch],
        cost_estimate=pl.CostEstimate(flops=flops, bytes_accessed=moved, transcendentals=0),
        compiler_params=pltpu.CompilerParams(vmem_limit_bytes=9 * 2**20),
    )(*args)


def exchange(parts, axis):
    return lax.all_to_all(parts, axis, 0, 0, tiled=True)


def spread(value, axis, n):
    return exchange(jnp.broadcast_to(value[None], (n,) + value.shape), axis)


def swap(value, axis, bit=1):
    n = 4 if axis == "x" else 2
    return lax.ppermute(value, axis, [(i, i ^ bit) for i in range(n)])


def width_to_tokens(inverse):
    pairs = []
    for c in range(2):
        for z in range(8):
            for yh in range(2):
                for x in range(4):
                    c2 = x >> 1
                    z2 = (c ^ c2) * 4 + yh * 2 + (x & 1)
                    a = ((c * 8 + z) * 2 + yh) * 4 + x
                    b = ((c2 * 8 + z2) * 2 + (z >> 2)) * 4 + (z & 3)
                    pairs.append((b, a) if inverse else (a, b))
    return pairs


def keep_pairs():
    pairs = []
    for yl in range(4):
        for c in range(2):
            for yh in range(2):
                for x in range(4):
                    yl2, yh2 = (yl & 2) + yh, yl & 1
                    c2, x2 = x >> 1, c * 2 + (x & 1)
                    a, b = ((yl * 2 + c) * 2 + yh) * 4 + x, ((yl2 * 2 + c2) * 2 + yh2) * 4 + x2
                    pairs.append((a, b))
    return pairs


def mm(a, b, ca, cb):
    return lax.dot_general(a, b, (((ca,), (cb,)), ((), ())), preferred_element_type=F32)


def copies_kernel(x_ref, out_ref):
    value = x_ref[...]
    for i in range(8):
        out_ref[i] = value


def copies2_kernel(x_ref, y_ref, out_ref):
    for k, ref in enumerate((x_ref, y_ref)):
        value = ref[...]
        for i in range(8):
            out_ref[i, k] = value


def hid_kernel(acts, wa, wb, out, rows):
    total = None
    for i, w in enumerate((wa, wb)):
        x = jnp.concatenate([acts[4 * i + t] for t in range(4)], axis=1)
        part = mm(w[...], x, 0, 0)
        total = part if total is None else total + part
    rows[0:HID, :] = total
    live = lax.broadcasted_iota(jnp.int32, (PAD, 512), 0) < BLK
    for a in range(2):
        for b in range(4):
            block = rows[pl.ds((a * 4 + b) * BLK, PAD), :]
            block = jnp.where(live, block, 0.0).astype(BF16)
            for t in range(4):
                out[(b & 2) + (t & 1), 4 * a + 2 * (b & 1) + (t >> 1)] = block[:, 128 * t : 128 * t + 128]


def grad_of(ga, gb):
    cols = [jnp.concatenate([g[j, k] for g in (ga, gb) for k in range(2)], axis=1) for j in range(8)]
    return jnp.concatenate(cols, axis=0)


def place(low, i):
    yh, x = lax.axis_index("yh"), lax.axis_index("x")
    return 4 * ((x // 2) ^ (i // 2)) + 2 * low + (yh ^ (i % 2))


def d_z_kernel(ga, gb, wa, wb, mine, other, blocks):
    c, low = lax.axis_index("c"), lax.axis_index("x") % 2
    grad = grad_of(ga, gb)
    for half, w in ((low, wa), (1 - low, wb)):
        part = mm(w[...], grad, 1, 0)
        part = jnp.concatenate([part, jnp.zeros((PAD - BLK, 512), F32)], axis=0)
        for i in range(4):
            blocks[place(half, i)] = part[:, 128 * i : 128 * i + 128]
    for i in range(4):
        mine[i] = blocks[4 * c + i]
        other[i] = blocks[4 * (1 - c) + i]


def sums_kernel(hid, d_z, d_z2, out):
    yh = lax.axis_index("yh")
    out[:, 1] = jnp.zeros((8, PAD, 128), BF16)
    for i in range(8):
        total = hid[0, i].astype(F32)
        for s in range(1, 4):
            total = total + hid[s, i].astype(F32)
        out[i, 0] = total.astype(BF16)
    for i in range(4):
        out[4 * yh + i, 1] = (d_z[i] + d_z2[i]).astype(BF16)


def epilogue_kernel(parts, keep_ref, out):
    hid, d_z = (
        sum((parts[s, i].astype(F32) for s in range(1, 8)), parts[0, i].astype(F32))
        for i in range(2)
    )
    keep = keep_ref[...].astype(F32) * (1.0 / 0.9)
    cdf = 0.5 * (1.0 + lax.erf(hid * 0.7071067811865476))
    pdf = jnp.exp(-0.5 * hid * hid) * 0.3989422804014327
    z_act = (hid * cdf * keep).astype(BF16)
    d_hid = (d_z * keep * (cdf + hid * pdf)).astype(BF16)
    for i in range(8):
        out[i, 0] = z_act
        out[i, 1] = d_hid


def split_kernel(both, z_act, d_hid):
    yh = lax.axis_index("yh")
    for i in range(4):
        z_act[i] = both[4 * yh + i, 0]
    for i in range(8):
        for x in range(4):
            d_hid[x, i] = both[i, 1]


def gather_rows(d_hid, rows, at):
    for a in range(2):
        for b in range(4):
            for t in range(4):
                rows[pl.ds((a * 4 + b) * BLK, PAD), at + 128 * t : at + 128 * t + 128] = d_hid[
                    (b & 2) + (t & 1), 4 * a + 2 * (b & 1) + (t >> 1)
                ].astype(F32)


def d_act_kernel(d_hid, wa, wb, out, rows):
    gather_rows(d_hid, rows, 0)
    d_hid = rows[0:HID, :].astype(BF16)
    for i, w in enumerate((wa, wb)):
        part = mm(w[...], d_hid, 1, 0).astype(BF16)
        for t in range(4):
            out[4 * i + t] = part[:, 128 * t : 128 * t + 128]


def d_act_sum_kernel(parts, out):
    total = parts[0].astype(F32)
    for s in range(1, 8):
        total = total + parts[s].astype(F32)
    out[...] = total.astype(BF16)


def d_win_kernel(acts, d_hid, mine, other, rows):
    gather_rows(d_hid, rows, 0)
    d_hid = rows[0:HID, :].astype(BF16)
    for i, out in enumerate((mine, other)):
        x = jnp.concatenate([acts[4 * i + t] for t in range(4)], axis=1)
        out[...] = mm(x, d_hid, 1, 1).astype(out.dtype)


def d_wout_kernel(z_act, z_act2, ga, gb, mine, other, z_all):
    c, low = lax.axis_index("c"), lax.axis_index("x") % 2
    for i in range(4):
        z_all[4 * c + i] = z_act[i]
        z_all[4 * (1 - c) + i] = z_act2[i]
    grad = grad_of(ga, gb)
    for half, out in ((low, mine), (1 - low, other)):
        z = [z_all[place(half, i)] for i in range(4)]
        part = mm(jnp.concatenate(z, axis=1), grad, 1, 1)[0:BLK]
        out[...] = part.astype(out.dtype)


def finish_kernel(mine, other, out):
    out[...] = (mine[...] + other[...].astype(F32)).astype(BF16)


def local(x_act, d_out, w_in, w_out, keep_mask):
    yl, c = lax.axis_index("yl"), lax.axis_index("c")
    y_ring = ("yh", "yl")
    hold = lax.optimization_barrier
    flops = 2 * 256 * HID * HID
    block = (PAD, 128)

    acts = lax.ppermute(x_act.T, ("c", "z", "yh", "x"), width_to_tokens(False))
    (grads,) = call(copies2_kernel, [((8, 2, SUB, 128), BF16)], d_out.T, swap(d_out.T, "yh"))
    grads = exchange(grads, "z")
    w_in2 = swap(w_in, "c")
    at = ((yl & 1) * 4 + 2 * c + (yl >> 1)) * BLK
    keep = lax.dynamic_slice(keep_mask, (0, at), (128, BLK)).astype(BF16).T
    keep = jnp.pad(keep, ((0, PAD - BLK), (0, 0)))
    keep = lax.ppermute(keep, ("yl", "c", "yh", "x"), keep_pairs())
    (acts,) = call(copies_kernel, [((8, SUB, 128), BF16)], acts)
    w_out2 = swap(w_out, "x")
    acts, grads, keep, w_in2, w_out2 = hold((acts, grads, keep, w_in2, w_out2))
    acts = exchange(acts, "z")
    grads2 = swap(grads, "x", 2)

    (hid,) = call(
        hid_kernel, [((4, 8) + block, BF16)], acts, w_in, w_in2, scratch=[((944, 512), F32)], flops=flops
    )
    hid, grads, grads2 = hold((hid, grads, grads2))
    hid = exchange(hid, "x")
    d_z, d_z2 = call(
        d_z_kernel, [((4,) + block, F32)] * 2, grads, grads2, w_out, w_out2,
        scratch=[((8,) + block, F32)], flops=flops,
    )
    (sums,) = call(sums_kernel, [((8, 2) + block, BF16)], hid, d_z, swap(d_z2, "c"))
    sums = exchange(sums, y_ring)
    (both,) = call(epilogue_kernel, [((8, 2) + block, BF16)], sums, keep)
    both = exchange(both, y_ring)
    z_act, d_hid = call(split_kernel, [((4,) + block, BF16), ((4, 8) + block, BF16)], both)
    d_hid = exchange(d_hid, "x")

    mine, other = call(
        d_wout_kernel,
        [((BLK, 2 * HID), F32), ((BLK, 2 * HID), BF16)],
        z_act, swap(z_act, "c"), grads, grads2, scratch=[((8,) + block, BF16)], flops=flops,
    )
    d_hid, other = hold((d_hid, other))
    (d_act,) = call(
        d_act_kernel, [((8, SUB, 128), BF16)], d_hid, w_in, w_in2, scratch=[((944, 512), F32)], flops=flops
    )
    d_act = exchange(d_act, "z")
    mine_in, other_in = call(
        d_win_kernel, [((SUB, HID), F32), ((SUB, HID), BF16)],
        acts, d_hid, scratch=[((944, 512), F32)], flops=flops,
    )
    (d_win,) = call(finish_kernel, [((SUB, HID), BF16)], mine_in, swap(other_in, "c"))
    d_act, d_win = hold((d_act, d_win))
    (d_act,) = call(d_act_sum_kernel, [((SUB, 128), BF16)], d_act)
    d_act = lax.ppermute(d_act, ("c", "z", "yh", "x"), width_to_tokens(True))
    (d_wout,) = call(finish_kernel, [((BLK, 2 * HID), BF16)], mine, swap(other, "x"))
    return d_act.T, d_win, d_wout


def solution(mesh):
    cube = Mesh(mesh.devices.reshape(4, 2, 8, 2, 4), ("yl", "c", "z", "yh", "x"))
    tokens, width = ("yh", "x"), ("yl", "c", "z")
    in_specs = (
        P(tokens, width),
        P(tokens, width),
        P(("yl", "c", "yh", "x"), "z"),
        P(("z", "yh", "x"), ("yl", "c")),
        P(tokens, "z"),
    )
    out_specs = (in_specs[0], in_specs[2], in_specs[3])
    return jax.shard_map(local, mesh=cube, in_specs=in_specs, out_specs=out_specs, check_vma=False)
```
